32 devices in a mesh: group: 2 (over x), fsdp: 2 (over core), tensor: 8 (over z, y).
Axes of the slice: x: 2, y: 2, z: 4, core: 2. Of those that a mesh axis runs over, the one named last changes fastest.
Arguments:
- row_states: bfloat16 [1024, 8192], P(('group', 'fsdp'), 'tensor'), parts along dimension 0, may hold values from -6 to 6
- norm_gain: float32 [8192], replicated, may hold values from 0.1 to 1.9
- exit_depth: int32 [1024], P(('group', 'fsdp')), parts along dimension 0, may hold values from 0 to 79
- gate_weight: bfloat16 [8192, 16384], P(None, ('fsdp', 'tensor')), may hold values from -0.0625 to 0.0625
- up_weight: bfloat16 [8192, 16384], P(None, ('fsdp', 'tensor')), may hold values from -0.0625 to 0.0625
- down_weight: bfloat16 [8192, 16384], P(None, ('fsdp', 'tensor')), may hold values from -0.0625 to 0.0625
- gate_delta: bfloat16 [8192, 16384], P(('fsdp', 'tensor')), may hold values from -4 to 4
- up_delta: bfloat16 [8192, 16384], P(('fsdp', 'tensor')), may hold values from -4 to 4
- down_delta: bfloat16 [8192, 16384], P(('fsdp', 'tensor')), may hold values from -4 to 4
- gate_index: int32 [128, 128], P(('fsdp', 'tensor')), may hold values from 0 to 255
- up_index: int32 [128, 128], P(('fsdp', 'tensor')), may hold values from 0 to 255
- down_index: int32 [128, 128], P(('fsdp', 'tensor')), may hold values from 0 to 255
- scale_table: float32 [256], replicated, may hold values from 0.002 to 0.01
Outputs:
- layer_out: bfloat16 [1024, 8192], P(('group', 'fsdp'), 'tensor'), parts along dimension 0
The draws below stay inside these ranges and needn't reach their ends.
There are 2 independent parts, one for each index of `group`. The reference program is written for one: setup_inputs(seed, part) draws one part's arguments, and reference() takes and returns one part's arrays. A program takes and returns all parts, laid end to end along the dimension named above; an argument that names none is the same for every part. Nothing has to cross between parts.
All inputs are finite; a program needn't handle non-finite values.
Results may differ from the reference program's by a relative error of at most 0.0023.
The reference program's roundings to bfloat16 on the way (of `fresh_gate`, `fresh_up`, `fresh_down`, `normed` and `hidden`) count: a program that leaves them out, or rounds other values in their place, can miss the bound.
Values may be sent and summed in bfloat16 or wider, within the bound.
A program may use at most 448 MiB of HBM per device.

```python
import math
import jax
import jax.numpy as jnp
from jax import lax

D = 8192
W = 16384
ROWS = 512
BLOCK_ROWS = 64
BLOCK_COLS = 128
NSCALE = 256
LAYER = 40
DEPTHS = 80


def with_ends(values, stream_key, least, top_value):
    spot = [jax.random.randint(jax.random.fold_in(stream_key, axis), (), 0, length) for axis, length in enumerate(values.shape)]
    main_axis = values.shape.index(max(values.shape))
    beside = spot[:main_axis] + [(spot[main_axis] + 1) % values.shape[main_axis]] + spot[main_axis + 1:]
    return values.at[tuple(spot)].set(least).at[tuple(beside)].set(top_value)


def spiked(entries, own_key, source, target, parts, factor):
    owner, partner = [(jnp.arange(entries.shape[dim]) // (entries.shape[dim] // parts)).reshape([-1 if axis == dim else 1 for axis in range(entries.ndim)]) for dim in (source, target)]
    chosen = jax.random.permutation(own_key, parts)[partner]
    strong = (owner == chosen) | (owner == (partner + parts // 2) % parts)
    return jnp.where(strong, factor * entries, entries)


def steps_of(stream_key, dims, split, low, top_value):
    def one(position, shards_of):
        heights = jax.random.uniform(jax.random.fold_in(jax.random.fold_in(stream_key, 6), position), (shards_of,), jnp.float32, low / len(split), top_value / len(split))
        return jnp.repeat(jnp.exp(heights), dims[position] // shards_of).reshape((-1,) + (1,) * (len(dims) - position - 1))

    gain = one(*split[0])
    for cut in split[1:]:
        gain = gain * one(*cut)
    return gain


def centred(stream_key, dims, spread, bound, split=(), dtype=jnp.bfloat16):
    gain = steps_of(stream_key, dims, split, -0.22, 0.18) if split else 1.0
    drawn = jax.random.normal(stream_key, dims, jnp.float32) * spread * gain
    return jnp.minimum(jnp.maximum(drawn, -bound), bound).astype(dtype)


def bell_draw_with(rng, shape, spread, most, pieces, heavy, kind=jnp.bfloat16):
    result = spread * jax.random.normal(rng, shape, jnp.float32)
    if pieces:
        result = result * steps_of(rng, shape, pieces, -0.22, 0.18)
    return jnp.clip(spiked(result, jax.random.fold_in(rng, 3), *heavy), -most, most).astype(kind)


def setup_inputs(seed: int = 0, part: int = 0) -> dict:
    seeds = jax.random.split(jax.random.key(seed), 14)
    own_keys = jax.random.split(jax.random.fold_in(seeds[13], part), 14)
    return {
        "row_states": centred(own_keys[0], (ROWS, D), 1.0, 6.0, ((0, 2), (1, 8))),
        "norm_gain": jnp.clip(1.0 + 0.18 * jax.random.normal(seeds[1], (D,), jnp.float32), 0.1, 1.9),
        "exit_depth": with_ends(jax.random.randint(own_keys[2], (ROWS,), 0, DEPTHS), jax.random.fold_in(own_keys[2], 1), 0, DEPTHS - 1).astype(jnp.int32),
        "gate_weight": centred(seeds[3], (D, W), D ** -0.5, 0.0625, ((1, 16),)),
        "up_weight": centred(seeds[4], (D, W), D ** -0.5, 0.0625, ((1, 16),)),
        "down_weight": bell_draw_with(seeds[5], (D, W), W ** -0.5, 0.0625, ((1, 16),), (1, 0, 16, 2.0)),
        "gate_delta": centred(seeds[6], (D, W), 1.0, 4.0, ((0, 16),)),
        "up_delta": centred(seeds[7], (D, W), 1.0, 4.0, ((0, 16),)),
        "down_delta": centred(seeds[8], (D, W), 1.0, 4.0, ((0, 16),)),
        "gate_index": with_ends(jax.random.randint(seeds[9], (D // BLOCK_ROWS, W // BLOCK_COLS), 0, NSCALE), jax.random.fold_in(seeds[9], 1), 0, NSCALE - 1).astype(jnp.int32),
        "up_index": with_ends(jax.random.randint(seeds[10], (D // BLOCK_ROWS, W // BLOCK_COLS), 0, NSCALE), jax.random.fold_in(seeds[10], 1), 0, NSCALE - 1).astype(jnp.int32),
        "down_index": with_ends(jax.random.randint(seeds[11], (D // BLOCK_ROWS, W // BLOCK_COLS), 0, NSCALE), jax.random.fold_in(seeds[11], 1), 0, NSCALE - 1).astype(jnp.int32),
        "scale_table": jnp.clip(jnp.exp(jax.random.uniform(seeds[12], (NSCALE,), jnp.float32, math.log(0.002), math.log(0.01))), 0.002, 0.01),
    }


def refresh(weight, delta, index, scale_table):
    block_count, col_blocks = index.shape
    total_rows, total_cols = weight.shape
    scales = scale_table[index]
    shaped = delta.astype(jnp.float32).reshape(block_count, total_rows // block_count, col_blocks, total_cols // col_blocks)
    update = (shaped * scales[:, None, :, None]).reshape(total_rows, total_cols)
    return (weight.astype(jnp.float32) + update).astype(jnp.bfloat16)

def reference(row_states, norm_gain, exit_depth, gate_weight, up_weight, down_weight, gate_delta, up_delta, down_delta, gate_index, up_index, down_index, scale_table):
    fresh_gate = refresh(gate_weight, gate_delta, gate_index, scale_table)
    fresh_up = refresh(up_weight, up_delta, up_index, scale_table)
    fresh_down = refresh(down_weight, down_delta, down_index, scale_table)
    values = row_states.astype(jnp.float32)
    mean_square = lax.optimization_barrier(jnp.mean(values * values, axis=-1, keepdims=True))
    normed = (values * lax.rsqrt(mean_square + 1e-05) * norm_gain.astype(jnp.float32)).astype(jnp.bfloat16)
    gate = jnp.dot(normed, fresh_gate, preferred_element_type=jnp.float32)
    up_part = jnp.dot(normed, fresh_up, preferred_element_type=jnp.float32)
    hidden = (jax.nn.silu(gate) * up_part).astype(jnp.bfloat16)
    ffn = jnp.dot(hidden, fresh_down.T, preferred_element_type=jnp.float32)
    active = (exit_depth > LAYER)[:, None]
    return (values + jnp.where(active, ffn, jnp.float32(0.0))).astype(jnp.bfloat16)
```

```python
import jax
import jax.numpy as jnp
from jax import lax
from jax.sharding import PartitionSpec as P

LAYER = 40
SHARDS = ("fsdp", "tensor")

epsilon = 1e-05


def block_scales(index_values, scale_table):
    entries = jnp.arange(scale_table.shape[0], dtype=jnp.int32)
    return jnp.sum(jnp.where(index_values[..., None] == entries, scale_table, jnp.float32(0.0)), axis=-1)


def land(delta, start, rows, shards):
    cols = delta.shape[1]
    part = lax.dynamic_slice_in_dim(delta, start, rows, axis=0)
    part = part.reshape(rows, shards, cols // shards).transpose(1, 0, 2)
    return lax.all_to_all(part, SHARDS, split_axis=0, concat_axis=0, tiled=True)


def refresh(weight, landed, scales):
    shards, rows, cols = landed.shape
    blocks, col_blocks = scales.shape[1:]
    shape = (shards, blocks, rows // blocks, col_blocks, cols // col_blocks)
    update = landed.astype(jnp.float32).reshape(shape) * scales[:, :, None, :, None]
    return (weight.astype(jnp.float32) + update.reshape(landed.shape)).astype(jnp.bfloat16)


def on_device(
    shards,
    groups,
    row_states,
    norm_gain,
    exit_depth,
    gate_weight,
    up_weight,
    down_weight,
    gate_delta,
    up_delta,
    down_delta,
    gate_index,
    up_index,
    down_index,
    scale_table,
):
    group = lax.axis_index("group")
    other = groups - 1 - group
    shard_rows = gate_delta.shape[0]
    half = shard_rows // groups
    cols = gate_weight.shape[1]
    block_rows = shard_rows // gate_index.shape[0]

    index = jnp.stack([gate_index, up_index, down_index], axis=1).astype(jnp.bfloat16)
    index = index.reshape(index.shape[0], 3, shards, -1).transpose(2, 1, 0, 3)
    index = lax.all_to_all(index, SHARDS, split_axis=0, concat_axis=0, tiled=True).astype(jnp.int32)
    scales = block_scales(index, scale_table)

    def swap(x):
        return lax.ppermute(x, "group", [(i, groups - 1 - i) for i in range(groups)])

    def fresh_part(weight, delta, which, offset, rows):
        start = group * half + offset
        landed = land(delta, start, rows, shards)
        view = weight.reshape(shards, shard_rows, cols)
        view = lax.dynamic_slice_in_dim(view, start, rows, axis=1)
        count = max(rows // block_rows, 1)
        part = lax.dynamic_slice_in_dim(scales[:, which], start // block_rows, count, axis=1)
        return refresh(view, landed, part)

    full_rows = lax.all_gather(row_states, "tensor", axis=1, tiled=True)
    values = full_rows.astype(jnp.float32)
    mean_square = jnp.mean(values * values, axis=-1, keepdims=True)
    normed = (values * lax.rsqrt(mean_square + epsilon) * norm_gain).astype(jnp.bfloat16)
    piece_rows = lax.all_gather(normed, "fsdp", axis=0, tiled=True)
    tokens = piece_rows.shape[0]
    split = piece_rows.reshape(tokens, shards, groups, half)

    def features(which):
        return lax.dynamic_index_in_dim(split, which, axis=2, keepdims=False).reshape(tokens, -1)

    mine_rows, other_rows = features(group), features(other)

    def project(weight, delta, which):
        mine = fresh_part(weight, delta, which, 0, half).reshape(-1, cols)
        theirs = swap(mine)
        return jnp.dot(mine_rows, mine, preferred_element_type=jnp.float32) + jnp.dot(
            other_rows, theirs, preferred_element_type=jnp.float32
        )

    gate_part = project(gate_weight, gate_delta, 0)
    up_part = project(up_weight, up_delta, 1)
    hidden = (jax.nn.silu(gate_part) * up_part).astype(jnp.bfloat16)

    def reduced(fresh):
        sums = lax.dot_general(
            hidden, fresh, (((1,), (1,)), ((), ())), preferred_element_type=jnp.float32
        )
        sums = lax.psum_scatter(sums, "fsdp", scatter_dimension=0, tiled=True)
        return lax.psum_scatter(sums, "tensor", scatter_dimension=1, tiled=True)

    pieces = 2
    rows = half // pieces
    own, far = [], []
    for piece in range(pieces):
        mine = fresh_part(down_weight, down_delta, 2, piece * rows, rows).reshape(-1, cols)
        theirs = swap(mine)
        own.append(reduced(mine))
        far.append(reduced(theirs))

    def joined(parts):
        return jnp.concatenate(
            [p.reshape(p.shape[0], -1, rows) for p in parts], axis=2
        )

    own, far = joined(own), joined(far)
    first = jnp.where(group == 0, own, far)
    second = jnp.where(group == 0, far, own)
    summed = jnp.stack([first, second], axis=2).reshape(row_states.shape)
    active = (exit_depth > LAYER)[:, None]
    return (row_states.astype(jnp.float32) + jnp.where(active, summed, jnp.float32(0.0))).astype(
        jnp.bfloat16
    )


def solution(mesh):
    shards = mesh.shape["fsdp"] * mesh.shape["tensor"]
    groups = mesh.shape["group"]

    def body(*arrays):
        return on_device(shards, groups, *arrays)

    in_specs = (
        P(("group", "fsdp"), "tensor"),
        P(),
        P(("group", "fsdp")),
        P(None, SHARDS),
        P(None, SHARDS),
        P(None, SHARDS),
        P(SHARDS, None),
        P(SHARDS, None),
        P(SHARDS, None),
        P(SHARDS, None),
        P(SHARDS, None),
        P(SHARDS, None),
        P(),
    )
    out_specs = P(("group", "fsdp"), "tensor")
    return jax.shard_map(body, mesh=mesh, in_specs=in_specs, out_specs=out_specs, check_vma=False)
```

```python
import jax
import jax.numpy as jnp
from jax import lax
from jax.sharding import PartitionSpec as P

LAYER = 40
SHARDS = ("fsdp", "tensor")

epsilon = 1e-05


def block_scales(index_values, scale_table):
    entries = jnp.arange(scale_table.shape[0], dtype=jnp.int32)
    return jnp.sum(jnp.where(index_values[..., None] == entries, scale_table, jnp.float32(0.0)), axis=-1)


def after(x, *deps):
    return lax.optimization_barrier((x,) + deps)[0]


def cut(part, shards):
    rows, cols = part.shape
    return part.reshape(rows, shards, cols // shards).transpose(1, 0, 2)


def refresh(weight, landed, scales):
    shards, rows, cols = landed.shape
    blocks, col_blocks = scales.shape[1:]
    shape = (shards, blocks, rows // blocks, col_blocks, cols // col_blocks)
    update = landed.astype(jnp.float32).reshape(shape) * scales[:, :, None, :, None]
    return (weight.astype(jnp.float32) + update.reshape(landed.shape)).astype(jnp.bfloat16)


def on_device(
    tensor,
    shards,
    groups,
    row_states,
    norm_gain,
    exit_depth,
    gate_weight,
    up_weight,
    down_weight,
    gate_delta,
    up_delta,
    down_delta,
    gate_index,
    up_index,
    down_index,
    scale_table,
):
    group = lax.axis_index("group")
    other = groups - 1 - group
    shard_rows = gate_delta.shape[0]
    half = shard_rows // groups
    cols = gate_weight.shape[1]
    block_rows = shard_rows // gate_index.shape[0]

    index = jnp.stack([gate_index, up_index, down_index], axis=1).astype(jnp.bfloat16)
    index = index.reshape(index.shape[0], 3, shards, -1).transpose(2, 1, 0, 3)
    index = lax.all_to_all(index, SHARDS, split_axis=0, concat_axis=0, tiled=True).astype(jnp.int32)
    scales = block_scales(index, scale_table)

    def swap(x):
        return lax.ppermute(x, "group", [(i, groups - 1 - i) for i in range(groups)])

    full_rows = lax.all_gather(row_states, "tensor", axis=1, tiled=True)
    values = full_rows.astype(jnp.float32)
    mean_square = jnp.mean(values * values, axis=-1, keepdims=True)
    normed = (values * lax.rsqrt(mean_square + epsilon) * norm_gain).astype(jnp.bfloat16)
    piece_rows = lax.all_gather(normed, "fsdp", axis=0, tiled=True)
    tokens = piece_rows.shape[0]
    split = piece_rows.reshape(tokens, shards, groups, half)

    def features(which, offset, rows):
        part = lax.dynamic_index_in_dim(split, which, axis=2, keepdims=False)
        return part[:, :, offset : offset + rows].reshape(tokens, -1)

    small = half // 2
    jobs = [
        (gate_weight, gate_delta, 0, 0, small),
        (gate_weight, gate_delta, 0, small, small),
        (up_weight, up_delta, 1, 0, small),
        (up_weight, up_delta, 1, small, small),
        (down_weight, down_delta, 2, 0, small),
        (down_weight, down_delta, 2, small, small),
    ]
    own, far = [], []
    previous = None
    for number, (weight, delta, which, offset, rows) in enumerate(jobs):
        start = group * half + offset
        part = lax.dynamic_slice_in_dim(delta, start, rows, axis=0)
        if number == 0:
            part = after(part, full_rows)
        elif number == 1:
            part = after(part, previous)
        elif number == 2:
            part = after(part, own[0])
        else:
            part = after(part, own[number - 2], far[number - 3])
        previous = cut(part, shards)
        landed = lax.all_to_all(previous, SHARDS, split_axis=0, concat_axis=0, tiled=True)
        if number:
            landed = after(landed, own[number - 1])
        view = weight.reshape(shards, shard_rows, cols)
        view = lax.dynamic_slice_in_dim(view, start, rows, axis=1)
        count = max(rows // block_rows, 1)
        part = lax.dynamic_slice_in_dim(scales[:, which], start // block_rows, count, axis=1)
        mine = refresh(view, landed, part).reshape(-1, cols)
        own.append(mine)
        far.append(swap(mine))

    def project(which):
        total = jnp.float32(0.0)
        for where, held in ((group, own), (other, far)):
            for (_, _, place, offset, rows), fresh in zip(jobs, held):
                if place == which:
                    total = total + jnp.dot(
                        features(where, offset, rows), fresh, preferred_element_type=jnp.float32
                    )
        return total

    gate_part = project(0)
    up_part = project(1)
    hidden = (jax.nn.silu(gate_part) * up_part).astype(jnp.bfloat16)

    def reduced(hidden, parts):
        sums = [
            lax.dot_general(
                hidden, fresh, (((1,), (1,)), ((), ())), preferred_element_type=jnp.float32
            ).reshape(tokens, tensor, -1)
            for fresh in parts
        ]
        sums = jnp.concatenate(sums, axis=2).reshape(tokens, -1)
        sums = lax.psum_scatter(sums, "fsdp", scatter_dimension=0, tiled=True)
        sums = lax.psum_scatter(sums, "tensor", scatter_dimension=1, tiled=True)
        sums = sums.reshape(sums.shape[0], len(parts), -1, small)
        return sums.transpose(0, 2, 1, 3).reshape(sums.shape[0], -1, half)

    own_sums = reduced(hidden, own[4:])
    far_sums = reduced(after(hidden, own_sums), far[4:])
    first = jnp.where(group == 0, own_sums, far_sums)
    second = jnp.where(group == 0, far_sums, own_sums)
    summed = jnp.stack([first, second], axis=2).reshape(row_states.shape)
    active = (exit_depth > LAYER)[:, None]
    return (row_states.astype(jnp.float32) + jnp.where(active, summed, jnp.float32(0.0))).astype(
        jnp.bfloat16
    )


def solution(mesh):
    shards = mesh.shape["fsdp"] * mesh.shape["tensor"]
    groups = mesh.shape["group"]

    def body(*arrays):
        return on_device(mesh.shape["tensor"], shards, groups, *arrays)

    in_specs = (
        P(("group", "fsdp"), "tensor"),
        P(),
        P(("group", "fsdp")),
        P(None, SHARDS),
        P(None, SHARDS),
        P(None, SHARDS),
        P(SHARDS, None),
        P(SHARDS, None),
        P(SHARDS, None),
        P(SHARDS, None),
        P(SHARDS, None),
        P(SHARDS, None),
        P(),
    )
    out_specs = P(("group", "fsdp"), "tensor")
    return jax.shard_map(body, mesh=mesh, in_specs=in_specs, out_specs=out_specs, check_vma=False)
```

```python
import jax
import jax.numpy as jnp
from jax import lax
from jax.sharding import PartitionSpec as P

LAYER = 40
SHARDS = ("fsdp", "tensor")

epsilon = 1e-05


def block_scales(index_values, scale_table):
    entries = jnp.arange(scale_table.shape[0], dtype=jnp.int32)
    return jnp.sum(jnp.where(index_values[..., None] == entries, scale_table, jnp.float32(0.0)), axis=-1)


def after(x, *deps):
    return lax.optimization_barrier((x,) + deps)[0]


def cut(part, shards):
    rows, cols = part.shape
    return part.reshape(rows, shards, cols // shards).transpose(1, 0, 2)


def refresh(weight, landed, scales):
    shards, rows, cols = landed.shape
    blocks, col_blocks = scales.shape[1:]
    shape = (shards, blocks, rows // blocks, col_blocks, cols // col_blocks)
    update = landed.astype(jnp.float32).reshape(shape) * scales[:, :, None, :, None]
    return (weight.astype(jnp.float32) + update.reshape(landed.shape)).astype(jnp.bfloat16)


def on_device(
    tensor,
    shards,
    groups,
    row_states,
    norm_gain,
    exit_depth,
    gate_weight,
    up_weight,
    down_weight,
    gate_delta,
    up_delta,
    down_delta,
    gate_index,
    up_index,
    down_index,
    scale_table,
):
    group = lax.axis_index("group")
    other = groups - 1 - group
    shard_rows = gate_delta.shape[0]
    half = shard_rows // groups
    cols = gate_weight.shape[1]
    block_rows = shard_rows // gate_index.shape[0]

    index = jnp.stack([gate_index, up_index, down_index], axis=1).astype(jnp.bfloat16)
    index = index.reshape(index.shape[0], 3, shards, -1).transpose(2, 1, 0, 3)
    index = lax.all_to_all(index, SHARDS, split_axis=0, concat_axis=0, tiled=True).astype(jnp.int32)
    scales = block_scales(index, scale_table)

    def swap(x):
        return lax.ppermute(x, "group", [(i, groups - 1 - i) for i in range(groups)])

    full_rows = lax.all_gather(row_states, "tensor", axis=1, tiled=True)
    values = full_rows.astype(jnp.float32)
    mean_square = jnp.mean(values * values, axis=-1, keepdims=True)
    normed = (values * lax.rsqrt(mean_square + epsilon) * norm_gain).astype(jnp.bfloat16)
    piece_rows = lax.all_gather(normed, "fsdp", axis=0, tiled=True)
    tokens = piece_rows.shape[0]
    split = piece_rows.reshape(tokens, shards, groups, half)

    def features(which, offset, rows):
        part = lax.dynamic_index_in_dim(split, which, axis=2, keepdims=False)
        return part[:, :, offset : offset + rows].reshape(tokens, -1)

    small = half // 2
    jobs = [
        (gate_weight, gate_delta, 0, 0, small),
        (gate_weight, gate_delta, 0, small, small),
        (up_weight, up_delta, 1, 0, small),
        (up_weight, up_delta, 1, small, small),
        (down_weight, down_delta, 2, 0, small),
        (down_weight, down_delta, 2, small, small),
    ]
    own, far = [], []
    previous = None
    for number, (weight, delta, which, offset, rows) in enumerate(jobs):
        start = group * half + offset
        part = lax.dynamic_slice_in_dim(delta, start, rows, axis=0)
        if number == 0:
            part = after(part, full_rows)
        elif number == 1:
            part = after(part, previous)
        elif number == 2:
            part = after(part, own[0])
        else:
            part = after(part, own[number - 2], far[number - 3])
        previous = cut(part, shards)
        landed = lax.all_to_all(previous, SHARDS, split_axis=0, concat_axis=0, tiled=True)
        if number:
            landed = after(landed, own[number - 1])
        view = weight.reshape(shards, shard_rows, cols)
        view = lax.dynamic_slice_in_dim(view, start, rows, axis=1)
        count = max(rows // block_rows, 1)
        part = lax.dynamic_slice_in_dim(scales[:, which], start // block_rows, count, axis=1)
        mine = refresh(view, landed, part).reshape(-1, cols)
        own.append(mine)
        far.append(swap(mine))

    def project(which):
        total = jnp.float32(0.0)
        for where, held in ((group, own), (other, far)):
            for (_, _, place, offset, rows), fresh in zip(jobs, held):
                if place == which:
                    total = total + jnp.dot(
                        features(where, offset, rows), fresh, preferred_element_type=jnp.float32
                    )
        return total

    gate_part = project(0)
    up_part = project(1)
    hidden = (jax.nn.silu(gate_part) * up_part).astype(jnp.bfloat16)

    def reduced(hidden, parts):
        sums = [
            lax.dot_general(
                hidden, fresh, (((1,), (1,)), ((), ())), preferred_element_type=jnp.float32
            ).reshape(tokens, tensor, -1)
            for fresh in parts
        ]
        sums = jnp.concatenate(sums, axis=2).reshape(tokens, -1)
        sums = lax.psum_scatter(sums, "fsdp", scatter_dimension=0, tiled=True)
        sums = lax.psum_scatter(sums, "tensor", scatter_dimension=1, tiled=True)
        sums = sums.reshape(sums.shape[0], len(parts), -1, small)
        return sums.transpose(0, 2, 1, 3).reshape(sums.shape[0], -1, half)

    own_sums = reduced(hidden, own[4:])
    held, own_sums = lax.optimization_barrier((far[4:], own_sums))
    far_sums = reduced(hidden, held)
    first = jnp.where(group == 0, own_sums, far_sums)
    second = jnp.where(group == 0, far_sums, own_sums)
    summed = jnp.stack([first, second], axis=2).reshape(row_states.shape)
    active = (exit_depth > LAYER)[:, None]
    return (row_states.astype(jnp.float32) + jnp.where(active, summed, jnp.float32(0.0))).astype(
        jnp.bfloat16
    )


def solution(mesh):
    shards = mesh.shape["fsdp"] * mesh.shape["tensor"]
    groups = mesh.shape["group"]

    def body(*arrays):
        return on_device(mesh.shape["tensor"], shards, groups, *arrays)

    in_specs = (
        P(("group", "fsdp"), "tensor"),
        P(),
        P(("group", "fsdp")),
        P(None, SHARDS),
        P(None, SHARDS),
        P(None, SHARDS),
        P(SHARDS, None),
        P(SHARDS, None),
        P(SHARDS, None),
        P(SHARDS, None),
        P(SHARDS, None),
        P(SHARDS, None),
        P(),
    )
    out_specs = P(("group", "fsdp"), "tensor")
    return jax.shard_map(body, mesh=mesh, in_specs=in_specs, out_specs=out_specs, check_vma=False)
```
